128 devices in a mesh: row: 8 (over x, core), col: 16 (over y, z).
Axes of the slice: x: 4, y: 4, z: 4, core: 2. Of those that a mesh axis runs over, the one named last changes fastest.
Arguments:
- hamiltonian: bfloat16 [5824, 5824], P('row', 'col'), may hold values from -6 to 6
- new_atom: int32 [448], replicated, may hold values from 0 to 447, as said below
- pattern: int32 [448, 448], P('row', 'col'), may hold values 0 or 1
Outputs:
- sign_matrix: float32 [5824, 5824], P('row', 'col')
The draws below stay inside these ranges and needn't reach their ends.
Inputs may be any that keep to these rules, and one draw needn't show every extreme that they name: `new_atom`: each old atom appears once. Block column b holds atoms b * 28 to (b + 1) * 28 - 1 in both orders. For each new block column d and each v from 0 to 27, exactly one atom of new block column d comes from old block column (d - 1 - (v mod 16)) mod 16, so the number of atoms that old block column b sends to new block column (b + k) mod 16 is the number of such v with (1 + v) mod 16 = k.
All inputs are finite; a program needn't handle non-finite values. No bound on the sum of `pattern` on one device may be relied on, other than what follows from the above.
Results may differ from the reference program's by a relative error of at most 0.0029.
Values may be sent and summed in bfloat16 or wider, within the bound.
No kernel may reach another device: no remote copies, remote signals or barrier semaphores. Data moves between devices by JAX's collectives and lax.ppermute only.
A program may use at most 64 MiB of HBM per device.

```python
import jax
import jax.numpy as jnp
from jax import lax

NBF = 13
ATOM_COL = 28
ATOMS = 448
ORDER = 5824
N_COL = 16


def draw_new_atom(key, part):
    slot_key, arrive_key = jax.random.split(jax.random.fold_in(key, 17))
    slot_keys = jax.random.split(slot_key, N_COL)
    arrive_keys = jax.random.split(arrive_key, N_COL)
    slot_inverse = jax.vmap(lambda k: jax.random.permutation(k, ATOM_COL))(slot_keys).astype(jnp.int32)
    arrival = jax.vmap(lambda k: jax.random.permutation(k, ATOM_COL))(arrive_keys).astype(jnp.int32)
    target = jnp.arange(N_COL, dtype=jnp.int32)[:, None]
    source = (target - 1 - arrival % N_COL) % N_COL
    old_atom = source * ATOM_COL + slot_inverse[source, arrival]
    return old_atom.reshape(-1).astype(jnp.int32)


def set_ends(result, key, smallest, top_value):
    dims = result.shape
    spot = [jax.random.randint(jax.random.fold_in(key, axis), (), 0, dims[axis]) for axis in range(len(dims))]
    result = result.at[tuple(spot)].set(smallest)
    longest = dims.index(max(dims))
    spot[longest] = (spot[longest] + 1) % dims[longest]
    return result.at[tuple(spot)].set(top_value)


def block_scale(key, dims, cuts, smallest, largest):
    gain, own = 1.0, jax.random.fold_in(key, 6)
    for dim, blocks in cuts:
        heights = jnp.exp(jax.random.uniform(jax.random.fold_in(own, dim), (blocks,), jnp.float32, smallest / len(cuts), largest / len(cuts)))
        gain = gain * jnp.repeat(heights, dims[dim] // blocks).reshape([-1 if axis == dim else 1 for axis in range(len(dims))])
    return gain


def normal_values(stream_key, dims, deviation, most, shards=(), held_as=jnp.bfloat16):
    result = jax.random.normal(stream_key, dims, jnp.float32) * deviation
    if len(shards) > 0:
        result = block_scale(stream_key, dims, shards, -0.22, 0.18) * result
    return jnp.clip(result, min=-most, max=most).astype(held_as)


def setup_inputs(seed: int = 0) -> dict:
    streams_of = jax.random.split(jax.random.key(seed), 4)
    hamiltonian = normal_values(streams_of[0], (ORDER, ORDER), 1.0, 6.0, ((0, 8), (1, 16)))
    new_atom = draw_new_atom(jax.random.fold_in(streams_of[3], 71), 0)
    pattern = set_ends((jax.random.randint(streams_of[2], (ATOMS, ATOMS), 0, 3) < 1).astype(jnp.int32), jax.random.fold_in(streams_of[2], 1), 0, 1)
    return dict(hamiltonian=hamiltonian, new_atom=new_atom, pattern=pattern)


def reference(hamiltonian, new_atom, pattern):
    order_all = ATOMS * NBF
    index = (new_atom[:, None] * NBF + jnp.arange(NBF, dtype=jnp.int32)[None, :]).reshape(-1).astype(jnp.int32)
    moved = jnp.take(jnp.take(hamiltonian, index, axis=0), index, axis=1)
    keep = jnp.broadcast_to(pattern.astype(jnp.float32)[:, None, :, None], (ATOMS, NBF, ATOMS, NBF)).reshape(order_all, order_all)
    masked = moved.astype(jnp.float32) * keep
    total = jnp.sum(masked * masked)
    start = (masked * lax.rsqrt(total / order_all)).astype(jnp.bfloat16)
    square = (jnp.dot(start, start, preferred_element_type=jnp.float32) * keep).astype(jnp.bfloat16)
    cube = jnp.dot(start, square, preferred_element_type=jnp.float32) * keep
    return keep * (1.5 * start.astype(jnp.float32) - 0.5 * cube)
```

```python
import functools

import jax
import jax.numpy as jnp
import numpy as np
from jax import lax
from jax.experimental import pallas as pl
from jax.experimental.pallas import tpu as pltpu
from jax.sharding import Mesh
from jax.sharding import PartitionSpec as P

NBF = 13
ROW = ("x", "c")
COL = ("y", "z")
BF = jnp.bfloat16
F32 = jnp.float32


def shift(n, by):
    return [(i, (i + by) % n) for i in range(n)]


def eq(left, right):
    return (left == right).astype(BF)


def exact(left, right, dims=(((1,), (0,)), ((), ()))):
    return lax.dot_general(left, right, dims, preferred_element_type=F32).astype(BF)


def slots_of(source, groups, per_group):
    same = source[:, :, None] == source[:, None, :]
    earlier = np.tril(np.ones((per_group, per_group), bool), -1)
    return jnp.sum((same & earlier[None]).astype(jnp.int32), axis=2)


def packed(new_atom, here, per_block, groups, slots):
    table = new_atom.reshape(groups, per_block)
    source = table // per_block
    rank = slots_of(source, groups, per_block)
    hit = (source == here)[:, None, :] & (rank[:, None, :] == np.arange(slots)[None, :, None])
    return jnp.sum(jnp.where(hit, (table - here * per_block)[:, None, :] + 1000, 0), axis=2) - 1000


def arrivals(new_atom, here, per_block):
    table = lax.dynamic_slice_in_dim(new_atom, here * per_block, per_block)
    source = table // per_block
    return source, slots_of(source[None], 1, per_block)[0]


def multiply(panel, mask, index, blocks, epilogue, extra, out_shape, start=None):
    _, parts, rows, depth = panel.shape
    count = len(blocks)
    cols = blocks[0].shape[-1]

    def body(index_ref, panel_ref, mask_ref, *refs):
        block_refs = refs[:count]
        rest = refs[count:-2]
        out_ref, acc = refs[-2:]
        if start is not None:
            start_ref, rest = rest[0], rest[1:]
        step = pl.program_id(0)

        @pl.when(step == 0)
        def _():
            acc[...] = jnp.zeros_like(acc) if start is None else start_ref[...]

        for j in range(count):

            @pl.when(step // 2 == j)
            def _(j=j):
                right = block_refs[j][step % 2]
                for part in range(parts):
                    left = panel_ref[0, part] * mask_ref[0, part]
                    acc[part] += jnp.dot(left, right, preferred_element_type=F32)

        @pl.when(step == 2 * count - 1)
        def _():
            epilogue(acc, out_ref, *rest)

    whole = pl.BlockSpec(memory_space=pltpu.VMEM)
    moving = pl.BlockSpec((1, parts, rows, depth), lambda g, index: (index[g], 0, 0, 0))
    operands = ([] if start is None else [start]) + [a for a, _ in extra]
    specs = ([] if start is None else [whole]) + [s for _, s in extra]
    flops = 2 * parts * rows * depth * cols * 2 * count
    return pl.pallas_call(
        body,
        out_shape=out_shape,
        grid_spec=pltpu.PrefetchScalarGridSpec(
            num_scalar_prefetch=1,
            grid=(2 * count,),
            in_specs=[moving, moving] + [whole] * count + specs,
            out_specs=whole,
            scratch_shapes=[pltpu.VMEM((parts, rows, cols), F32)],
        ),
        compiler_params=pltpu.CompilerParams(vmem_limit_bytes=40 * 2**20),
        cost_estimate=pl.CostEstimate(
            flops=flops, bytes_accessed=count * 4 * parts * rows * depth * 2, transcendentals=0
        ),
    )(index, panel, mask, *blocks, *operands)


def square_end(acc, out_ref, keep_ref, scale_ref):
    scale = scale_ref[0, 0]
    for part in range(acc.shape[0]):
        value = (acc[part] * scale) * scale * keep_ref[part].astype(F32)
        out_ref[part] = value.astype(BF)


def keep_sum(acc, out_ref):
    out_ref[...] = acc[...]


def sign_end(acc, out_ref, keep_ref, moved_ref, scale_ref, pack_ref):
    scale = scale_ref[0, 0]
    packed_rows = None
    for part in range(acc.shape[0]):
        value = 1.5 * (moved_ref[part].astype(F32) * scale) - 0.5 * (acc[part] * scale)
        value = (value * keep_ref[part].astype(F32)).astype(BF)
        term = jnp.dot(pack_ref[part], value, preferred_element_type=F32)
        packed_rows = term if packed_rows is None else packed_rows + term
    out_ref[...] = packed_rows.astype(BF)


def unpack_body(place_ref, arrived_ref, out_ref):
    out_ref[...] = jnp.dot(place_ref[...], arrived_ref[...], preferred_element_type=F32)


def ring_near(block):
    before = lax.ppermute(block, "x", shift(4, 1))
    after = lax.ppermute(block, "x", shift(4, 3))
    own = lax.ppermute(block, "c", shift(2, 1))
    return before, after, own


def ring_far(before, after):
    first = lax.ppermute(before[0:1], "x", shift(4, 1))
    second = lax.ppermute(after[1:2], "x", shift(4, 3))
    return first, second


def other(array):
    return lax.ppermute(array, "c", shift(2, 1))


def column_panel(block):
    before, after, own_other = ring_near(block)
    first, second = ring_far(before, after)
    near = [block, before, after, own_other, other(before), other(after)]
    far = [(first, second), (other(first), other(second))]
    return near, [jnp.concatenate(pair, axis=0) for pair in far]


def on_device(hamiltonian, new_atom, pattern):
    rows_here, cols_here = hamiltonian.shape
    row_count, col_count = 8, 16
    atoms_row, atoms_col = pattern.shape
    atoms = atoms_col * col_count
    parts = rows_here // cols_here
    order_all = rows_here * row_count
    slots_col = -(-atoms_col // col_count)
    counts = np.bincount((1 + np.arange(atoms_col)) % col_count, minlength=col_count)
    targets = (np.arange(2)[:, None] + np.arange(col_count)[None, :]) % col_count // 2
    slots_row = max(
        int(np.sum((targets == t) * counts[None, :])) for t in range(row_count)
    )
    x, c = lax.axis_index("x"), lax.axis_index("c")
    row_here = 2 * x + c
    col_here = lax.axis_index(COL)
    h_parts = hamiltonian.reshape(parts, cols_here, cols_here)
    panel = lax.all_gather(h_parts, COL, axis=0)

    wide = 32
    q = np.arange(wide)
    base = packed(new_atom, col_here, atoms_col, col_count, slots_col)
    column = jnp.where(
        (q < slots_col * NBF)[None, :],
        jnp.repeat(base * NBF, NBF, axis=1, total_repeat_length=slots_col * NBF)[
            :, np.minimum(q, slots_col * NBF - 1)
        ]
        + (q % NBF)[None, :],
        -1,
    ).reshape(-1)
    pick = eq(column[:, None], np.arange(cols_here)[None, :])
    outgoing = exact(pick, hamiltonian, (((1,), (1,)), ((), ())))
    arrived = lax.all_to_all(
        outgoing.reshape(col_count, wide, rows_here), COL, 0, 0
    ).reshape(col_count * wide, rows_here)
    source, rank = arrivals(new_atom, col_here, atoms_col)
    spot = ((source * wide + rank * NBF)[:, None] + np.arange(NBF)[None, :]).reshape(-1)
    place = eq(np.arange(col_count * wide)[:, None], spot[None, :])
    moved = exact(arrived, place, (((0,), (0,)), ((), ())))

    strip = lax.all_gather(pattern.astype(BF), ROW, axis=0, tiled=True)
    old_row = row_here * atoms_row + np.arange(atoms_row)
    rows_pattern = exact(eq(old_row[:, None], new_atom[None, :]), strip)
    tall = eq(np.arange(rows_here)[:, None] // NBF, np.arange(atoms_row)[None, :])
    broad = eq(np.arange(atoms_col)[:, None], np.arange(cols_here)[None, :] // NBF)
    keep = exact(exact(tall, rows_pattern), broad)
    right = moved * keep
    keep = keep.reshape(parts, cols_here, cols_here)
    right = right.reshape(parts, cols_here, cols_here)
    near, far = column_panel(right)

    part_sum = jnp.sum(jnp.square(right.astype(F32)))
    sent = jnp.concatenate(
        [rows_pattern.astype(F32), jnp.broadcast_to(part_sum, (8, atoms_col))], axis=0
    )
    seen = lax.all_gather(lax.all_gather(sent, "z", axis=0), "y", axis=0)
    seen = seen.reshape(col_count, atoms_row + 8, atoms_col)
    total = lax.psum(lax.psum(jnp.sum(seen[:, atoms_row, 0]), "c"), "x")
    scale = lax.rsqrt(total / order_all).reshape(1, 1)
    all_cols = jnp.transpose(seen[:, :atoms_row], (1, 0, 2)).reshape(atoms_row, atoms).astype(BF)
    old_col = np.arange(order_all) // NBF
    wide_pattern = exact(all_cols, eq(new_atom[:, None], old_col[None, :]))
    wide_pattern = wide_pattern.reshape(atoms_row, col_count, cols_here)
    tall_parts = tall.reshape(parts, cols_here, atoms_row)
    mask = jnp.einsum(
        "pra,acn->cprn", tall_parts, wide_pattern, preferred_element_type=F32
    ).astype(BF)

    def rho(dx, other_core):
        return 2 * jnp.mod(x + dx, 4) + jnp.mod(c + other_core, 2)

    def blocks_of(places):
        return jnp.stack([2 * rho(dx, oc) + t for dx, oc in places for t in range(2)]).astype(
            jnp.int32
        )

    near_places = [(0, 0), (-1, 0), (1, 0), (0, 1), (-1, 1), (1, 1)]
    far_places = [(2, 0), (2, 1)]
    near_index, far_index = blocks_of(near_places), blocks_of(far_places)
    all_index = jnp.concatenate([near_index, far_index])
    whole = pl.BlockSpec(memory_space=pltpu.VMEM)
    scalar = pl.BlockSpec(memory_space=pltpu.SMEM)
    shape = (parts, cols_here, cols_here)
    square = multiply(
        panel, mask, all_index, near + far, square_end,
        [(keep, whole), (scale, scalar)], jax.ShapeDtypeStruct(shape, BF),
    )
    near, far = column_panel(square)
    partial = multiply(
        panel, mask, near_index, near, keep_sum, [], jax.ShapeDtypeStruct(shape, F32)
    )
    base = packed(new_atom, row_here, atoms_row, row_count, slots_row)
    line = (base[:, :, None] * NBF + np.arange(NBF)).reshape(-1)
    pack_rows = eq(line[None, :, None], np.arange(rows_here).reshape(parts, 1, cols_here))
    sent_rows = multiply(
        panel, mask, far_index, far, sign_end,
        [(keep, whole), (right, whole), (scale, scalar), (pack_rows, whole)],
        jax.ShapeDtypeStruct((row_count * slots_row * NBF, cols_here), BF),
        start=partial,
    )
    got_rows = lax.all_to_all(
        sent_rows.reshape(row_count, slots_row * NBF, cols_here), ROW, 0, 0
    ).reshape(-1, cols_here)
    source, rank = arrivals(new_atom, row_here, atoms_row)
    spot = (((source * slots_row + rank) * NBF)[:, None] + np.arange(NBF)).reshape(-1)
    place_rows = eq(spot[:, None], np.arange(row_count * slots_row * NBF)[None, :])
    return pl.pallas_call(
        unpack_body,
        out_shape=jax.ShapeDtypeStruct((rows_here, cols_here), F32),
        in_specs=[whole, whole],
        out_specs=whole,
    )(place_rows, got_rows)


def solution(mesh):
    split = Mesh(mesh.devices.reshape(4, 2, 4, 4), ("x", "c", "y", "z"))
    return jax.shard_map(
        on_device,
        mesh=split,
        in_specs=(P(ROW, COL), P(), P(ROW, COL)),
        out_specs=P(ROW, COL),
        check_vma=False,
    )
```

```python
import functools

import jax
import jax.numpy as jnp
import numpy as np
from jax import lax
from jax.experimental import pallas as pl
from jax.experimental.pallas import tpu as pltpu
from jax.sharding import Mesh
from jax.sharding import PartitionSpec as P

NBF = 13
ROW = ("x", "c")
COL = ("y", "z")
BF = jnp.bfloat16
F32 = jnp.float32


def shift(n, by):
    return [(i, (i + by) % n) for i in range(n)]


def eq(left, right):
    return (left == right).astype(BF)


def exact(left, right, dims=(((1,), (0,)), ((), ()))):
    return lax.dot_general(left, right, dims, preferred_element_type=F32).astype(BF)


def slots_of(source, groups, per_group):
    same = source[:, :, None] == source[:, None, :]
    earlier = np.tril(np.ones((per_group, per_group), bool), -1)
    return jnp.sum((same & earlier[None]).astype(jnp.int32), axis=2)


def packed(new_atom, here, per_block, groups, slots):
    table = new_atom.reshape(groups, per_block)
    source = table // per_block
    rank = slots_of(source, groups, per_block)
    hit = (source == here)[:, None, :] & (rank[:, None, :] == np.arange(slots)[None, :, None])
    return jnp.sum(jnp.where(hit, (table - here * per_block)[:, None, :] + 1000, 0), axis=2) - 1000


def arrivals(new_atom, here, per_block):
    table = lax.dynamic_slice_in_dim(new_atom, here * per_block, per_block)
    source = table // per_block
    return source, slots_of(source[None], 1, per_block)[0]


TALL = 368
WIDE = 384


def multiply(panel, tall, wide, scale, index, blocks, scaled, epilogue, extra, out_shape, start=None):
    count = len(blocks)
    rows = panel.shape[1]

    def body(index_ref, scale_ref, panel_ref, tall_ref, wide_ref, *refs):
        block_refs = refs[: 2 * count]
        out_refs, acc = refs[-1 - len(out_shape) : -1], refs[-1]
        rest = refs[2 * count : -1 - len(out_shape)]
        if start is not None:
            start_ref, rest = rest[0], rest[1:]
        step = pl.program_id(0)
        by = scale_ref[0, 0]

        @pl.when(step == 0)
        def _():
            acc[...] = jnp.zeros_like(acc) if start is None else start_ref[...]

        kept = jnp.dot(tall_ref[...], wide_ref[0], preferred_element_type=F32) * by
        left = jnp.concatenate([panel_ref[0], panel_ref[1]], axis=1)
        left = (left.astype(F32) * kept).astype(BF)
        gap = jnp.zeros((WIDE - TALL, WIDE), BF)
        for j in range(count):

            @pl.when(step == j)
            def _(j=j):
                top, bottom = block_refs[2 * j][...], block_refs[2 * j + 1][...]
                if scaled:
                    top = (top.astype(F32) * by).astype(BF)
                    bottom = (bottom.astype(F32) * by).astype(BF)
                right = jnp.concatenate([top, gap, bottom, gap], axis=0)
                acc[...] += jnp.dot(left, right, preferred_element_type=F32)

        @pl.when(step == count - 1)
        def _():
            epilogue(acc, by, out_refs, *rest)

    whole = pl.BlockSpec(memory_space=pltpu.VMEM)
    operands = [b for pair in blocks for b in pair] + ([] if start is None else [start]) + extra
    return pl.pallas_call(
        body,
        out_shape=out_shape,
        grid_spec=pltpu.PrefetchScalarGridSpec(
            num_scalar_prefetch=1,
            grid=(count,),
            in_specs=[
                pl.BlockSpec(memory_space=pltpu.SMEM),
                pl.BlockSpec((2, rows, WIDE), lambda g, index: (index[g], 0, 0)),
                whole,
                pl.BlockSpec((1,) + wide.shape[1:], lambda g, index: (index[g], 0, 0)),
            ]
            + [whole] * len(operands),
            out_specs=[whole] * len(out_shape),
            scratch_shapes=[pltpu.VMEM((rows, WIDE), F32)],
        ),
        compiler_params=pltpu.CompilerParams(vmem_limit_bytes=40 * 2**20),
        cost_estimate=pl.CostEstimate(
            flops=2 * rows * 2 * WIDE * WIDE * count,
            bytes_accessed=count * 3 * rows * WIDE * 2,
            transcendentals=0,
        ),
    )(index, scale, panel, tall, wide, *operands)


def square_end(acc, by, out_refs, keep_ref):
    for part in range(2):
        at = pl.ds(part * TALL, TALL)
        out_refs[part][...] = (acc[at, :] * keep_ref[at, :].astype(F32)).astype(BF)


def keep_sum(acc, by, out_refs):
    out_refs[0][...] = acc[...]


def sign_end(acc, by, out_refs, keep_ref, top_ref, bottom_ref, pack_ref):
    first = jnp.concatenate([top_ref[...], bottom_ref[...]], axis=0)
    first = (first.astype(F32) * by).astype(BF).astype(F32)
    value = (keep_ref[...].astype(F32) * (1.5 * first - 0.5 * acc[...])).astype(BF)
    out_refs[0][...] = jnp.dot(pack_ref[...], value, preferred_element_type=F32).astype(BF)


def unpack_body(place_ref, arrived_ref, out_ref):
    value = jnp.dot(place_ref[...], arrived_ref[...], preferred_element_type=F32)
    out_ref[...] = value[:, : out_ref.shape[1]]


def send(array, axis, by):
    return lax.ppermute(array, axis, shift(2 if axis == "c" else 4, by))


def around(array, axis):
    return [array] + [send(array, axis, by) for by in (1, 2, 3)]


def column_panel(top, bottom):
    before = (send(top, "x", 1), send(bottom, "x", 1))
    after = (send(top, "x", 3), send(bottom, "x", 3))
    opposite = (send(before[0], "x", 1), send(after[1], "x", 3))
    near = [(top, bottom), before, after]
    near = near + [tuple(send(half, "c", 1) for half in pair) for pair in near]
    far = [opposite, tuple(send(half, "c", 1) for half in opposite)]
    return near, far


def on_device(hamiltonian, new_atom, pattern):
    rows_here, cols_here = hamiltonian.shape
    row_count, col_count = 8, 16
    atoms_row, atoms_col = pattern.shape
    order_all = rows_here * row_count
    slots_col = -(-atoms_col // col_count)
    counts = np.bincount((1 + np.arange(atoms_col)) % col_count, minlength=col_count)
    targets = (np.arange(2)[:, None] + np.arange(col_count)[None, :]) % col_count // 2
    slots_row = max(int(np.sum((targets == t) * counts[None, :])) for t in range(row_count))
    x, c = lax.axis_index("x"), lax.axis_index("c")
    y, z = lax.axis_index("y"), lax.axis_index("z")
    row_here, col_here = 2 * x + c, 4 * y + z
    half = rows_here // 2
    pads = ((0, TALL - half), (0, WIDE - cols_here))
    padded = jnp.concatenate([jnp.pad(hamiltonian[:half], pads), jnp.pad(hamiltonian[half:], pads)])
    panel = lax.all_gather(padded, COL, axis=0)

    width = 32
    base = packed(new_atom, col_here, atoms_col, col_count, slots_col)
    spots = (base[:, :, None] * NBF + np.arange(NBF)).reshape(col_count, slots_col * NBF)
    column = jnp.pad(spots, ((0, 0), (0, width - slots_col * NBF)), constant_values=-1).reshape(-1)
    pick = eq(column[:, None], np.arange(WIDE)[None, :])
    outgoing = exact(pick, padded, (((1,), (1,)), ((), ())))
    arrived = lax.all_to_all(outgoing.reshape(col_count, width, 2 * TALL), COL, 0, 0)
    arrived = arrived.reshape(col_count * width, 2 * TALL)
    source, rank = arrivals(new_atom, col_here, atoms_col)
    spot = ((source * width + rank * NBF)[:, None] + np.arange(NBF)[None, :]).reshape(-1)
    spot = jnp.pad(spot, (0, WIDE - cols_here), constant_values=-1)
    place = eq(np.arange(col_count * width)[:, None], spot[None, :])
    moved = exact(arrived, place, (((0,), (0,)), ((), ())))

    own = pattern.astype(BF)
    strip = jnp.stack(around(jnp.stack([own, send(own, "c", 1)]), "x"))
    strip = strip.reshape(-1, atoms_col)
    rows_seen = jnp.stack([2 * jnp.mod(x - d, 4) + jnp.mod(c + o, 2) for d in range(4) for o in range(2)])
    atoms_seen = new_atom.reshape(row_count, atoms_row)[rows_seen].reshape(-1)
    old_row = row_here * atoms_row + np.arange(atoms_row)
    rows_pattern = exact(eq(old_row[:, None], atoms_seen[None, :]), strip)
    line = np.arange(2 * TALL) % TALL
    of_row = np.where(line < half, (np.arange(2 * TALL) // TALL * half + line) // NBF, -1)
    of_col = np.where(np.arange(WIDE) < cols_here, np.arange(WIDE) // NBF, -1)
    tall = eq(jnp.asarray(of_row)[:, None], np.arange(64)[None, :])
    broad = eq(np.arange(atoms_col)[:, None], jnp.asarray(of_col)[None, :])
    keep = exact(exact(tall[:, :atoms_row], rows_pattern), broad)
    right = moved * keep
    top, bottom = right[:TALL], right[TALL:]
    near, far = column_panel(top, bottom)

    part_sum = jnp.sum(jnp.square(right.astype(F32)))
    sent = jnp.concatenate(
        [rows_pattern.astype(F32), jnp.broadcast_to(part_sum, (8, atoms_col))], axis=0
    )
    seen = jnp.stack(around(jnp.stack(around(sent, "z")), "y"))
    seen = seen.reshape(col_count, atoms_row + 8, atoms_col)
    total = jnp.broadcast_to(jnp.sum(seen[:, atoms_row, 0]), (8, 128))
    total = total + send(total, "c", 1)
    total = sum(around(total, "x"))[:1, :1]
    scale = lax.rsqrt(total / order_all)
    cols_seen = jnp.stack([4 * jnp.mod(y - a, 4) + jnp.mod(z - b, 4) for a in range(4) for b in range(4)])
    atoms_seen = new_atom.reshape(col_count, atoms_col)[cols_seen].reshape(-1)
    all_cols = jnp.transpose(seen[:, :atoms_row], (1, 0, 2)).reshape(atoms_row, -1).astype(BF)
    all_cols = jnp.pad(all_cols, ((0, 64 - atoms_row), (0, 0)))
    old_col = np.where(of_col >= 0, np.arange(col_count)[:, None] * atoms_col + of_col, -1)
    old_col = jnp.asarray(old_col.reshape(row_count, 1, 2 * WIDE))
    wide = jnp.einsum(
        "ia,ran->rin", all_cols, eq(atoms_seen[None, :, None], old_col), preferred_element_type=F32
    ).astype(BF)

    def rho(step, other_core):
        return 2 * jnp.mod(x + step, 4) + jnp.mod(c + other_core, 2)

    near_index = jnp.stack([rho(d, o) for o in range(2) for d in (0, -1, 1)])
    far_index = jnp.stack([rho(2, o) for o in range(2)])
    half_block = jax.ShapeDtypeStruct((TALL, WIDE), BF)
    whole = pl.BlockSpec(memory_space=pltpu.VMEM)
    of_panel = functools.partial(multiply, panel, tall, wide, scale)
    square = of_panel(
        jnp.concatenate([near_index, far_index]), near + far, True, square_end, [keep], [half_block] * 2
    )
    near, far = column_panel(*square)
    partial = of_panel(
        near_index, near, False, keep_sum, [], [jax.ShapeDtypeStruct((2 * TALL, WIDE), F32)]
    )[0]
    base = packed(new_atom, row_here, atoms_row, row_count, slots_row)
    line = (base[:, :, None] * NBF + np.arange(NBF)).reshape(-1)
    row_of = np.where(of_row >= 0, np.arange(2 * TALL) - (np.arange(2 * TALL) // TALL) * (TALL - half), -1)
    pack_rows = eq(line[:, None], jnp.asarray(row_of)[None, :])
    sent_rows = of_panel(
        far_index, far, False, sign_end, [keep, top, bottom, pack_rows],
        [jax.ShapeDtypeStruct((row_count * slots_row * NBF, WIDE), BF)],
        start=partial,
    )[0]
    got_rows = lax.all_to_all(sent_rows.reshape(row_count, slots_row * NBF, WIDE), ROW, 0, 0)
    got_rows = got_rows.reshape(-1, WIDE)
    source, rank = arrivals(new_atom, row_here, atoms_row)
    spot = (((source * slots_row + rank) * NBF)[:, None] + np.arange(NBF)).reshape(-1)
    place_rows = eq(spot[:, None], np.arange(row_count * slots_row * NBF)[None, :])
    return pl.pallas_call(
        unpack_body,
        out_shape=jax.ShapeDtypeStruct((rows_here, cols_here), F32),
        in_specs=[whole, whole],
        out_specs=whole,
    )(place_rows, got_rows)


def solution(mesh):
    split = Mesh(mesh.devices.reshape(4, 2, 4, 4), ("x", "c", "y", "z"))
    return jax.shard_map(
        on_device,
        mesh=split,
        in_specs=(P(ROW, COL), P(), P(ROW, COL)),
        out_specs=P(ROW, COL),
        check_vma=False,
    )
```

```python
import functools

import jax
import jax.numpy as jnp
import numpy as np
from jax import lax
from jax.experimental import pallas as pl
from jax.experimental.pallas import tpu as pltpu
from jax.sharding import Mesh
from jax.sharding import PartitionSpec as P

NBF = 13
ROW = ("x", "c")
COL = ("y", "z")
BF = jnp.bfloat16
F32 = jnp.float32


def shift(n, by):
    return [(i, (i + by) % n) for i in range(n)]


def eq(left, right):
    return (left == right).astype(BF)


def exact(left, right, dims=(((1,), (0,)), ((), ()))):
    return lax.dot_general(left, right, dims, preferred_element_type=F32).astype(BF)


def slots_of(source, groups, per_group):
    same = source[:, :, None] == source[:, None, :]
    earlier = np.tril(np.ones((per_group, per_group), bool), -1)
    return jnp.sum((same & earlier[None]).astype(jnp.int32), axis=2)


def packed(new_atom, here, per_block, groups, slots):
    table = new_atom.reshape(groups, per_block)
    source = table // per_block
    rank = slots_of(source, groups, per_block)
    hit = (source == here)[:, None, :] & (rank[:, None, :] == np.arange(slots)[None, :, None])
    return jnp.sum(jnp.where(hit, (table - here * per_block)[:, None, :] + 1000, 0), axis=2) - 1000


def arrivals(new_atom, here, per_block):
    table = lax.dynamic_slice_in_dim(new_atom, here * per_block, per_block)
    source = table // per_block
    return source, slots_of(source[None], 1, per_block)[0]


TALL = 368
WIDE = 384


def multiply(panel, tall, wide, scale, index, blocks, scaled, epilogue, extra, out_shape, micros):
    count = len(blocks)
    rows = panel.shape[1]
    flat = [(j, piece) for j, pieces in enumerate(blocks) for piece in pieces]
    starts = [sum(p.shape[0] for _, p in flat[:k]) for k in range(len(flat))]
    halves = [
        (k, j, (at - 2 * TALL * j) // TALL, t)
        for k, ((j, piece), at) in enumerate(zip(flat, starts))
        for t in range(piece.shape[0] // TALL)
    ]

    def body(index_ref, scale_ref, panel_ref, tall_ref, wide_ref, *refs):
        pieces, refs = refs[: len(flat)], refs[len(flat) :]
        more, refs = refs[: len(extra)], refs[len(extra) :]
        outs, refs = refs[: len(out_shape)], refs[len(out_shape) :]
        acc, held, strips, sem, strip_sem, more_sem = refs[:6]
        kept_more = refs[6:]
        by = scale_ref[0, 0]

        def fetch(k, j, first, t):
            spot = held.at[j, pl.ds((first + t) * WIDE, TALL)]
            source = pieces[k].at[pl.ds(t * TALL, TALL)]
            return pltpu.make_async_copy(source, spot, sem.at[j, first + t])

        def fetch_strip(j):
            source = panel_ref.at[pl.ds(2 * index_ref[j], 2)]
            return pltpu.make_async_copy(source, strips.at[j], strip_sem.at[j])

        def fetch_more(k):
            return pltpu.make_async_copy(more[k], kept_more[k], more_sem.at[k])

        step = pl.program_id(0)

        @pl.when(step == 0)
        def _():
            for j in range(count):
                for one in halves:
                    if one[1] == j:
                        fetch(*one).start()
                fetch_strip(j).start()
            for k in range(len(extra)):
                fetch_more(k).start()
            acc[...] = jnp.zeros_like(acc)
            gap = jnp.zeros((WIDE - TALL, WIDE), BF)
            for j in range(count):
                for t in range(2):
                    held[j, t * WIDE + TALL : (t + 1) * WIDE] = gap

        kept = jnp.dot(tall_ref[...], wide_ref[index_ref[step]], preferred_element_type=F32)
        for j in range(count):

            @pl.when(step == j)
            def _(j=j):
                fetch_strip(j).wait()
                for one in halves:
                    if one[1] == j:
                        fetch(*one).wait()

        left = jnp.concatenate([strips[step, 0], strips[step, 1]], axis=1)
        left = (left.astype(F32) * (kept * by)).astype(BF)
        right = held[step]
        if scaled:
            right = (right.astype(F32) * by).astype(BF)
        acc[...] += jnp.dot(left, right, preferred_element_type=F32)

        @pl.when(step == count - 1)
        def _():
            for k in range(len(extra)):
                fetch_more(k).wait()
            epilogue(acc, by, outs, *kept_more)

    whole = pl.BlockSpec(memory_space=pltpu.VMEM)
    smem = pl.BlockSpec(memory_space=pltpu.SMEM)
    anywhere = pl.BlockSpec(memory_space=pltpu.HBM)
    operands = [piece for _, piece in flat] + extra
    return pl.pallas_call(
        body,
        out_shape=out_shape,
        grid=(count,),
        in_specs=[smem, smem, anywhere, whole, whole] + [anywhere] * len(operands),
        out_specs=[whole] * len(out_shape),
        scratch_shapes=[
            pltpu.VMEM((rows, WIDE), F32),
            pltpu.VMEM((count, 2 * WIDE, WIDE), BF),
            pltpu.VMEM((count, 2, rows, WIDE), BF),
            pltpu.SemaphoreType.DMA((count, 2)),
            pltpu.SemaphoreType.DMA((count,)),
            pltpu.SemaphoreType.DMA((max(len(extra), 1),)),
        ]
        + [pltpu.VMEM(e.shape, e.dtype) for e in extra],
        compiler_params=pltpu.CompilerParams(vmem_limit_bytes=60 * 2**20),
        cost_estimate=pl.CostEstimate(
            flops=int(micros * 1.15e9), bytes_accessed=int(micros * 3e6), transcendentals=0
        ),
    )(index, scale, panel, tall, wide, *operands)


def square_end(acc, by, outs, keep):
    outs[0][...] = (acc[...] * keep[...].astype(F32)).astype(BF)


def first_sum(acc, by, outs):
    outs[0][...] = acc[...]


def sign_end(acc, by, outs, so_far, keep, right, pack):
    first = (right[...].astype(F32) * by).astype(BF).astype(F32)
    cube = acc[...] + so_far[...]
    value = (keep[...].astype(F32) * (1.5 * first - 0.5 * cube)).astype(BF)
    outs[0][...] = jnp.dot(pack[...], value, preferred_element_type=F32).astype(BF)


def unpack_body(place_ref, arrived_ref, out_ref):
    value = jnp.dot(place_ref[...], arrived_ref[...], preferred_element_type=F32)
    out_ref[...] = value[:, : out_ref.shape[1]]


def after(ready, arrays):
    anywhere = pl.BlockSpec(memory_space=pl.ANY)
    return pl.pallas_call(
        lambda *refs: None,
        out_shape=[jax.ShapeDtypeStruct(a.shape, a.dtype) for a in arrays],
        in_specs=[anywhere] * (len(arrays) + 1),
        out_specs=[anywhere] * len(arrays),
        input_output_aliases={k + 1: k for k in range(len(arrays))},
    )(ready, *arrays)


def send(array, axis, by):
    return lax.ppermute(array, axis, shift(2 if axis == "c" else 4, by))


def around(array, axis):
    return [array] + [send(array, axis, by) for by in (1, 2, 3)]


def column_panel(block, beside=None):
    before, behind = send(block, "x", 1), send(block, "x", 3)
    opposite = [send(before[:TALL], "x", 1), send(behind[TALL:], "x", 3)]
    near = [(block,), (before,), (behind,)]
    near = near + [(send(one, "c", 1),) for one, in near]
    partial = None
    if beside is not None:
        partial = beside(near)
        opposite = after(partial, opposite)
    far = [tuple(opposite), tuple(send(half, "c", 1) for half in opposite)]
    return near, far, partial


def on_device(hamiltonian, new_atom, pattern):
    rows_here, cols_here = hamiltonian.shape
    row_count, col_count = 8, 16
    atoms_row, atoms_col = pattern.shape
    order_all = rows_here * row_count
    slots_col = -(-atoms_col // col_count)
    counts = np.bincount((1 + np.arange(atoms_col)) % col_count, minlength=col_count)
    targets = (np.arange(2)[:, None] + np.arange(col_count)[None, :]) % col_count // 2
    slots_row = max(int(np.sum((targets == t) * counts[None, :])) for t in range(row_count))
    x, c = lax.axis_index("x"), lax.axis_index("c")
    y, z = lax.axis_index("y"), lax.axis_index("z")
    row_here, col_here = 2 * x + c, 4 * y + z
    half = rows_here // 2
    pads = ((0, TALL - half), (0, WIDE - cols_here))
    padded = jnp.concatenate([jnp.pad(hamiltonian[:half], pads), jnp.pad(hamiltonian[half:], pads)])
    panel = lax.all_gather(padded, COL, axis=0)

    width = 32
    base = packed(new_atom, col_here, atoms_col, col_count, slots_col)
    spots = (base[:, :, None] * NBF + np.arange(NBF)).reshape(col_count, slots_col * NBF)
    column = jnp.pad(spots, ((0, 0), (0, width - slots_col * NBF)), constant_values=-1).reshape(-1)
    pick = eq(column[:, None], np.arange(WIDE)[None, :])
    outgoing = exact(pick, padded, (((1,), (1,)), ((), ())))
    arrived = lax.all_to_all(outgoing.reshape(col_count, width, 2 * TALL), COL, 0, 0)
    arrived = arrived.reshape(col_count * width, 2 * TALL)
    source, rank = arrivals(new_atom, col_here, atoms_col)
    spot = ((source * width + rank * NBF)[:, None] + np.arange(NBF)[None, :]).reshape(-1)
    spot = jnp.pad(spot, (0, WIDE - cols_here), constant_values=-1)
    place = eq(np.arange(col_count * width)[:, None], spot[None, :])
    moved = exact(arrived, place, (((0,), (0,)), ((), ())))

    own = pattern.astype(BF)
    strip = jnp.stack(around(jnp.stack([own, send(own, "c", 1)]), "x"))
    strip = strip.reshape(-1, atoms_col)
    rows_seen = jnp.stack([2 * jnp.mod(x - d, 4) + jnp.mod(c + o, 2) for d in range(4) for o in range(2)])
    atoms_seen = new_atom.reshape(row_count, atoms_row)[rows_seen].reshape(-1)
    old_row = row_here * atoms_row + np.arange(atoms_row)
    rows_pattern = exact(eq(old_row[:, None], atoms_seen[None, :]), strip)
    line = np.arange(2 * TALL) % TALL
    of_row = np.where(line < half, (np.arange(2 * TALL) // TALL * half + line) // NBF, -1)
    of_col = np.where(np.arange(WIDE) < cols_here, np.arange(WIDE) // NBF, -1)
    tall = eq(jnp.asarray(of_row)[:, None], np.arange(64)[None, :])
    broad = eq(np.arange(atoms_col)[:, None], jnp.asarray(of_col)[None, :])
    keep = exact(exact(tall[:, :atoms_row], rows_pattern), broad)
    right = moved * keep
    near, far, _ = column_panel(right)

    part_sum = jnp.sum(jnp.square(right[TALL:].astype(F32)))
    part_sum += jnp.sum(jnp.square(near[1][0][:TALL].astype(F32)))
    sent = jnp.concatenate(
        [rows_pattern.astype(F32), jnp.broadcast_to(part_sum, (8, atoms_col))], axis=0
    )
    seen = jnp.stack(around(jnp.stack(around(sent, "z")), "y"))
    seen = seen.reshape(col_count, atoms_row + 8, atoms_col)
    total = jnp.broadcast_to(jnp.sum(seen[:, atoms_row, 0]), (8, 128))
    total = total + send(total, "c", 1)
    total = sum(around(total, "x"))
    scale = lax.rsqrt(total[:1, :1] / order_all)
    cols_seen = jnp.stack([4 * jnp.mod(y - a, 4) + jnp.mod(z - b, 4) for a in range(4) for b in range(4)])
    atoms_seen = new_atom.reshape(col_count, atoms_col)[cols_seen].reshape(-1)
    all_cols = jnp.transpose(seen[:, :atoms_row], (1, 0, 2)).reshape(atoms_row, -1).astype(BF)
    all_cols = jnp.pad(all_cols, ((0, 64 - atoms_row), (0, 0)))
    old_col = np.where(of_col >= 0, np.arange(col_count)[:, None] * atoms_col + of_col, -1)
    old_col = jnp.asarray(old_col.reshape(row_count, 1, 2 * WIDE))
    wide = jnp.einsum(
        "ia,ran->rin", all_cols, eq(atoms_seen[None, :, None], old_col), preferred_element_type=F32
    ).astype(BF)

    def rho(step, other_core):
        return 2 * jnp.mod(x + step, 4) + jnp.mod(c + other_core, 2)

    near_index = jnp.stack([rho(d, o) for o in range(2) for d in (0, -1, 1)])
    far_index = jnp.stack([rho(2, o) for o in range(2)])
    sums = jax.ShapeDtypeStruct((2 * TALL, WIDE), F32)
    whole = pl.BlockSpec(memory_space=pltpu.VMEM)
    of_panel = functools.partial(multiply, panel, tall, wide, scale)
    all_index = jnp.concatenate([near_index, far_index])
    block = jax.ShapeDtypeStruct((2 * TALL, WIDE), BF)
    square = of_panel(all_index, near + far, True, square_end, [keep], [block], 9)[0]
    _, far, partial = column_panel(
        square, lambda near: of_panel(near_index, near, False, first_sum, [], [sums], 11)[0]
    )
    base = packed(new_atom, row_here, atoms_row, row_count, slots_row)
    line = (base[:, :, None] * NBF + np.arange(NBF)).reshape(-1)
    row_of = np.where(of_row >= 0, np.arange(2 * TALL) - (np.arange(2 * TALL) // TALL) * (TALL - half), -1)
    pack_rows = eq(line[:, None], jnp.asarray(row_of)[None, :])
    sent_rows = of_panel(
        far_index, far, False, sign_end, [partial, keep, right, pack_rows],
        [jax.ShapeDtypeStruct((row_count * slots_row * NBF, WIDE), BF)], 4,
    )[0]
    got_rows = lax.all_to_all(sent_rows.reshape(row_count, slots_row * NBF, WIDE), ROW, 0, 0)
    got_rows = got_rows.reshape(-1, WIDE)
    source, rank = arrivals(new_atom, row_here, atoms_row)
    spot = (((source * slots_row + rank) * NBF)[:, None] + np.arange(NBF)).reshape(-1)
    place_rows = eq(spot[:, None], np.arange(row_count * slots_row * NBF)[None, :])
    return pl.pallas_call(
        unpack_body,
        out_shape=jax.ShapeDtypeStruct((rows_here, cols_here), F32),
        in_specs=[whole, whole],
        out_specs=whole,
    )(place_rows, got_rows)


def solution(mesh):
    split = Mesh(mesh.devices.reshape(4, 2, 4, 4), ("x", "c", "y", "z"))
    return jax.shard_map(
        on_device,
        mesh=split,
        in_specs=(P(ROW, COL), P(), P(ROW, COL)),
        out_specs=P(ROW, COL),
        check_vma=False,
    )
```

```python
import functools

import jax
import jax.numpy as jnp
import numpy as np
from jax import lax
from jax.experimental import pallas as pl
from jax.experimental.pallas import tpu as pltpu
from jax.sharding import Mesh
from jax.sharding import PartitionSpec as P

NBF = 13
ROW = ("x", "c")
COL = ("y", "z")
BF = jnp.bfloat16
F32 = jnp.float32


def shift(n, by):
    return [(i, (i + by) % n) for i in range(n)]


def eq(left, right):
    return (left == right).astype(BF)


def exact(left, right, dims=(((1,), (0,)), ((), ()))):
    return lax.dot_general(left, right, dims, preferred_element_type=F32).astype(BF)


def slots_of(source, groups, per_group):
    same = source[:, :, None] == source[:, None, :]
    earlier = np.tril(np.ones((per_group, per_group), bool), -1)
    return jnp.sum((same & earlier[None]).astype(jnp.int32), axis=2)


def packed(new_atom, here, per_block, groups, slots):
    table = new_atom.reshape(groups, per_block)
    source = table // per_block
    rank = slots_of(source, groups, per_block)
    hit = (source == here)[:, None, :] & (rank[:, None, :] == np.arange(slots)[None, :, None])
    return jnp.sum(jnp.where(hit, (table - here * per_block)[:, None, :] + 1000, 0), axis=2) - 1000


def arrivals(new_atom, here, per_block):
    table = lax.dynamic_slice_in_dim(new_atom, here * per_block, per_block)
    source = table // per_block
    return source, slots_of(source[None], 1, per_block)[0]


TALL = 368
WIDE = 384


def mask_rows(strips, step, wide_ref, at, left):
    columns = left.shape[1]
    line = lax.broadcasted_iota(jnp.int32, (8, columns), 0)
    in_half = wide_ref.shape[1] // 2

    def of_atom(half, atom):
        return jnp.broadcast_to(wide_ref[at, pl.ds(half * in_half + atom, 1), :], (8, columns))

    for start in range(0, left.shape[0], 16):
        masks = []
        for first in (start, start + 8):
            half, row = divmod(first, TALL)
            atom, more = divmod(row, NBF)
            here = NBF - more
            mask = of_atom(half, atom)
            if here < 8:
                mask = jnp.where(line < here, mask, of_atom(half, atom + 1) if atom + 1 < in_half else 0.0)
            masks.append(mask)
        rows = pl.ds(start, 16)
        both = jnp.concatenate([strips[step, 0, rows], strips[step, 1, rows]], axis=1)
        left[rows] = (both.astype(F32) * jnp.concatenate(masks, axis=0)).astype(BF)


def multiply(panel, wide, scale, index, base, blocks, scaled, epilogue, extra, out_shape, micros, early=()):
    count = len(blocks)
    rows = panel.shape[1]
    flat = [(j, piece) for j, pieces in enumerate(blocks) for piece in pieces]
    starts = [sum(p.shape[0] for _, p in flat[:k]) for k in range(len(flat))]
    halves = [
        (k, j, (at - 2 * TALL * j) // TALL, t)
        for k, ((j, piece), at) in enumerate(zip(flat, starts))
        for t in range(piece.shape[0] // TALL)
    ]

    def body(index_ref, scale_ref, panel_ref, wide_ref, *refs):
        pieces, refs = refs[: len(flat)], refs[len(flat) :]
        more, refs = refs[: len(extra)], refs[len(extra) + len(early) :]
        outs, refs = refs[: len(out_shape)], refs[len(out_shape) :]
        acc, held, strips, left, sem, strip_sem, more_sem = refs[:7]
        kept_more = refs[7:]
        by = scale_ref[0, 0]

        def fetch(k, j, first, t):
            spot = held.at[j, pl.ds((first + t) * WIDE, TALL)]
            source = pieces[k].at[pl.ds(t * TALL, TALL)]
            return pltpu.make_async_copy(source, spot, sem.at[j, first + t])

        def fetch_strip(j):
            source = panel_ref.at[pl.ds(2 * index_ref[base + j], 2)]
            return pltpu.make_async_copy(source, strips.at[j], strip_sem.at[j])

        def fetch_more(k):
            return pltpu.make_async_copy(more[k], kept_more[k], more_sem.at[k])

        step = pl.program_id(0)

        @pl.when(step == 0)
        def _():
            for j in range(count):
                for one in halves:
                    if one[1] == j:
                        fetch(*one).start()
                fetch_strip(j).start()
            for k in range(len(extra)):
                fetch_more(k).start()
            acc[...] = jnp.zeros_like(acc)
            gap = jnp.zeros((WIDE - TALL, WIDE), BF)
            for j in range(count):
                for t in range(2):
                    held[j, t * WIDE + TALL : (t + 1) * WIDE] = gap

        for j in range(count):

            @pl.when(step == j)
            def _(j=j):
                fetch_strip(j).wait()
                for one in halves:
                    if one[1] == j:
                        fetch(*one).wait()

        mask_rows(strips, step, wide_ref, index_ref[base + step], left)
        right = held[step]
        if scaled:
            right = (right.astype(F32) * by).astype(BF)
        acc[...] += jnp.dot(left[...], right, preferred_element_type=F32)

        @pl.when(step == count - 1)
        def _():
            for k in range(len(extra)):
                fetch_more(k).wait()
            epilogue(acc, by, outs, *kept_more)

    whole = pl.BlockSpec(memory_space=pltpu.VMEM)
    smem = pl.BlockSpec(memory_space=pltpu.SMEM)
    anywhere = pl.BlockSpec(memory_space=pltpu.HBM)
    operands = [piece for _, piece in flat] + extra + list(early)
    return pl.pallas_call(
        body,
        out_shape=out_shape,
        grid=(count,),
        in_specs=[smem, smem, anywhere, whole] + [anywhere] * len(operands),
        out_specs=[whole] * len(out_shape),
        scratch_shapes=[
            pltpu.VMEM((rows, WIDE), F32),
            pltpu.VMEM((count, 2 * WIDE, WIDE), BF),
            pltpu.VMEM((count, 2, rows, WIDE), BF),
            pltpu.VMEM((rows, 2 * WIDE), BF),
            pltpu.SemaphoreType.DMA((count, 2)),
            pltpu.SemaphoreType.DMA((count,)),
            pltpu.SemaphoreType.DMA((max(len(extra), 1),)),
        ]
        + [pltpu.VMEM(e.shape, e.dtype) for e in extra],
        compiler_params=pltpu.CompilerParams(vmem_limit_bytes=60 * 2**20),
        cost_estimate=pl.CostEstimate(
            flops=int(micros * 1.15e9), bytes_accessed=int(micros * 3e6), transcendentals=0
        ),
    )(index, scale, panel, wide, *operands)


def square_end(acc, by, outs, keep):
    outs[0][...] = (acc[...] * keep[...].astype(F32)).astype(BF)


def first_sum(acc, by, outs):
    outs[0][...] = acc[...]


def sign_end(acc, by, outs, so_far, keep, right, pack):
    first = (right[...].astype(F32) * by).astype(BF).astype(F32)
    cube = acc[...] + so_far[...]
    value = (keep[...].astype(F32) * (1.5 * first - 0.5 * cube)).astype(BF)
    outs[0][...] = jnp.dot(pack[...], value, preferred_element_type=F32).astype(BF)


def unpack_body(place_ref, arrived_ref, out_ref):
    value = jnp.dot(place_ref[...], arrived_ref[...], preferred_element_type=F32)
    out_ref[...] = value[:, : out_ref.shape[1]]


def after(ready, arrays):
    anywhere = pl.BlockSpec(memory_space=pl.ANY)
    return pl.pallas_call(
        lambda *refs: None,
        out_shape=[jax.ShapeDtypeStruct(a.shape, a.dtype) for a in arrays],
        in_specs=[anywhere] * (len(arrays) + 1),
        out_specs=[anywhere] * len(arrays),
        input_output_aliases={k + 1: k for k in range(len(arrays))},
    )(ready, *arrays)


def send(array, axis, by):
    return lax.ppermute(array, axis, shift(2 if axis == "c" else 4, by))


def from_all(array, axes, count):
    return lax.all_to_all(jnp.broadcast_to(array[None], (count,) + array.shape), axes, 0, 0)


def column_panel(block, beside=None):
    before, behind = send(block, "x", 1), send(block, "x", 3)
    opposite = [send(before[:TALL], "x", 1), send(behind[TALL:], "x", 3)]
    near = [(one,) for first in (block, before, behind) for one in (first, send(first, "c", 1))]
    partial = None
    if beside is not None:
        partial = beside(near)
        opposite = after(partial, opposite)
    far = [tuple(opposite), tuple(send(half, "c", 1) for half in opposite)]
    return near, far, partial


def on_device(hamiltonian, new_atom, pattern):
    rows_here, cols_here = hamiltonian.shape
    row_count, col_count = 8, 16
    atoms_row, atoms_col = pattern.shape
    order_all = rows_here * row_count
    slots_col = -(-atoms_col // col_count)
    counts = np.bincount((1 + np.arange(atoms_col)) % col_count, minlength=col_count)
    targets = (np.arange(2)[:, None] + np.arange(col_count)[None, :]) % col_count // 2
    slots_row = max(int(np.sum((targets == t) * counts[None, :])) for t in range(row_count))
    x, c = lax.axis_index("x"), lax.axis_index("c")
    y, z = lax.axis_index("y"), lax.axis_index("z")
    row_here, col_here = 2 * x + c, 4 * y + z
    half = rows_here // 2
    pads = ((0, TALL - half), (0, WIDE - cols_here))
    padded = jnp.concatenate([jnp.pad(hamiltonian[:half], pads), jnp.pad(hamiltonian[half:], pads)])
    panel = lax.all_gather(padded, COL, axis=0)

    width = 32
    base = packed(new_atom, col_here, atoms_col, col_count, slots_col)
    spots = (base[:, :, None] * NBF + np.arange(NBF)).reshape(col_count, slots_col * NBF)
    column = jnp.pad(spots, ((0, 0), (0, width - slots_col * NBF)), constant_values=-1).reshape(-1)
    pick = eq(column[:, None], np.arange(WIDE)[None, :])
    outgoing = exact(pick, padded, (((1,), (1,)), ((), ())))
    arrived = lax.all_to_all(outgoing.reshape(col_count, width, 2 * TALL), COL, 0, 0)
    arrived = arrived.reshape(col_count * width, 2 * TALL)
    source, rank = arrivals(new_atom, col_here, atoms_col)
    spot = ((source * width + rank * NBF)[:, None] + np.arange(NBF)[None, :]).reshape(-1)
    spot = jnp.pad(spot, (0, WIDE - cols_here), constant_values=-1)
    place = eq(np.arange(col_count * width)[:, None], spot[None, :])
    moved = exact(arrived, place, (((0,), (0,)), ((), ())))

    strip = from_all(pattern.astype(BF), ROW, row_count).reshape(-1, atoms_col)
    old_row = row_here * atoms_row + np.arange(atoms_row)
    rows_pattern = exact(eq(old_row[:, None], new_atom[None, :]), strip)
    line = np.arange(2 * TALL) % TALL
    of_row = np.where(line < half, (np.arange(2 * TALL) // TALL * half + line) // NBF, -1)
    of_col = np.where(np.arange(WIDE) < cols_here, np.arange(WIDE) // NBF, -1)
    tall = eq(jnp.asarray(of_row)[:, None], np.arange(64)[None, :])
    broad = eq(np.arange(atoms_col)[:, None], jnp.asarray(of_col)[None, :])
    keep = exact(exact(tall[:, :atoms_row], rows_pattern), broad)
    right = moved * keep
    near, far, _ = column_panel(right)

    part_sum = jnp.sum(jnp.square(right.astype(F32)))
    sent = jnp.concatenate(
        [rows_pattern.astype(F32), jnp.broadcast_to(part_sum, (8, atoms_col))], axis=0
    )
    seen = from_all(sent, COL, col_count)
    total = jnp.broadcast_to(jnp.sum(seen[:, atoms_row, 0]), (8, 128))
    total = jnp.sum(from_all(total, ROW, row_count), axis=0)
    scale = lax.rsqrt(total[:1, :1] / order_all)
    all_cols = jnp.transpose(seen[:, :atoms_row], (1, 0, 2)).reshape(atoms_row, -1).astype(BF)
    old_col = np.where(of_col >= 0, np.arange(col_count)[:, None] * atoms_col + of_col, -1)
    old_col = jnp.asarray(old_col.reshape(row_count, 1, 2 * WIDE))
    wide = scale * jnp.einsum(
        "ia,ran->rin", all_cols, eq(new_atom[None, :, None], old_col), preferred_element_type=F32
    )

    def rho(step, other_core):
        return 2 * jnp.mod(x + step, 4) + jnp.mod(c + other_core, 2)

    index = jnp.stack([rho(d, o) for d in (0, -1, 1, 2) for o in range(2)])
    sums = jax.ShapeDtypeStruct((2 * TALL, WIDE), F32)
    whole = pl.BlockSpec(memory_space=pltpu.VMEM)
    of_panel = functools.partial(multiply, panel, wide, scale, index)
    base = packed(new_atom, row_here, atoms_row, row_count, slots_row)
    line = (base[:, :, None] * NBF + np.arange(NBF)).reshape(-1)
    row_of = np.where(of_row >= 0, np.arange(2 * TALL) - (np.arange(2 * TALL) // TALL) * (TALL - half), -1)
    pack_rows = eq(line[:, None], jnp.asarray(row_of)[None, :])
    block = jax.ShapeDtypeStruct((2 * TALL, WIDE), BF)
    square = of_panel(0, near + far, True, square_end, [keep], [block], 9, [pack_rows])[0]
    _, far, partial = column_panel(
        square, lambda near: of_panel(0, near, False, first_sum, [], [sums], 11)[0]
    )
    sent_rows = of_panel(
        6, far, False, sign_end, [partial, keep, right, pack_rows],
        [jax.ShapeDtypeStruct((row_count * slots_row * NBF, WIDE), BF)], 7,
    )[0]
    got_rows = lax.all_to_all(sent_rows.reshape(row_count, slots_row * NBF, WIDE), ROW, 0, 0)
    got_rows = got_rows.reshape(-1, WIDE)
    source, rank = arrivals(new_atom, row_here, atoms_row)
    spot = (((source * slots_row + rank) * NBF)[:, None] + np.arange(NBF)).reshape(-1)
    place_rows = eq(spot[:, None], np.arange(row_count * slots_row * NBF)[None, :])
    return pl.pallas_call(
        unpack_body,
        out_shape=jax.ShapeDtypeStruct((rows_here, cols_here), F32),
        in_specs=[whole, whole],
        out_specs=whole,
    )(place_rows, got_rows)


def solution(mesh):
    split = Mesh(mesh.devices.reshape(4, 2, 4, 4), ("x", "c", "y", "z"))
    return jax.shard_map(
        on_device,
        mesh=split,
        in_specs=(P(ROW, COL), P(), P(ROW, COL)),
        out_specs=P(ROW, COL),
        check_vma=False,
    )
```

```python
import functools

import jax
import jax.numpy as jnp
import numpy as np
from jax import lax
from jax.experimental import pallas as pl
from jax.experimental.pallas import tpu as pltpu
from jax.sharding import Mesh
from jax.sharding import PartitionSpec as P

NBF = 13
ROW = ("x", "c")
COL = ("y", "z")
BF = jnp.bfloat16
F32 = jnp.float32


def shift(n, by):
    return [(i, (i + by) % n) for i in range(n)]


def eq(left, right):
    return (left == right).astype(BF)


def exact(left, right, dims=(((1,), (0,)), ((), ()))):
    return lax.dot_general(left, right, dims, preferred_element_type=F32).astype(BF)


def slots_of(source, groups, per_group):
    same = source[:, :, None] == source[:, None, :]
    earlier = np.tril(np.ones((per_group, per_group), bool), -1)
    return jnp.sum((same & earlier[None]).astype(jnp.int32), axis=2)


def packed(new_atom, here, per_block, groups, slots):
    table = new_atom.reshape(groups, per_block)
    source = table // per_block
    rank = slots_of(source, groups, per_block)
    hit = (source == here)[:, None, :] & (rank[:, None, :] == np.arange(slots)[None, :, None])
    return jnp.sum(jnp.where(hit, (table - here * per_block)[:, None, :] + 1000, 0), axis=2) - 1000


def arrivals(new_atom, here, per_block):
    table = lax.dynamic_slice_in_dim(new_atom, here * per_block, per_block)
    source = table // per_block
    return source, slots_of(source[None], 1, per_block)[0]


TALL = 368
WIDE = 384


def mask_rows(strips, wides, step, left, first_column):
    columns = 2 * WIDE
    line = lax.broadcasted_iota(jnp.int32, (8, columns), 0)
    in_half = wides.shape[1] // 2

    def of_atom(half, atom):
        return jnp.broadcast_to(wides[step, pl.ds(half * in_half + atom, 1), :], (8, columns))

    for start in range(0, left.shape[0], 16):
        masks = []
        for first in (start, start + 8):
            half, row = divmod(first, TALL)
            atom, more = divmod(row, NBF)
            here = NBF - more
            mask = of_atom(half, atom)
            if here < 8:
                mask = jnp.where(line < here, mask, of_atom(half, atom + 1) if atom + 1 < in_half else 0.0)
            masks.append(mask)
        rows = pl.ds(start, 16)
        both = jnp.concatenate([strips[step, 0, rows], strips[step, 1, rows]], axis=1)
        left[rows, first_column : first_column + columns] = (both.astype(F32) * jnp.concatenate(masks, axis=0)).astype(BF)


def multiply(panel, wide, scale, index, base, blocks, scaled, epilogue, extra, out_shape, micros, early=()):
    count = len(blocks)
    rows = panel.shape[1]
    flat = [(j, piece) for j, pieces in enumerate(blocks) for piece in pieces]
    starts = [sum(p.shape[0] for _, p in flat[:k]) for k in range(len(flat))]
    halves = [
        (k, j, (at - 2 * TALL * j) // TALL, t)
        for k, ((j, piece), at) in enumerate(zip(flat, starts))
        for t in range(piece.shape[0] // TALL)
    ]

    def body(index_ref, scale_ref, panel_ref, wide_ref, *refs):
        pieces, refs = refs[: len(flat)], refs[len(flat) :]
        more, refs = refs[: len(extra)], refs[len(extra) + len(early) :]
        outs, refs = refs[: len(out_shape)], refs[len(out_shape) :]
        acc, held, strips, wides, left, sem, strip_sem, more_sem = refs[:8]
        kept_more = refs[8:]
        by = scale_ref[0, 0]

        def fetch(k, j, first, t):
            spot = held.at[j, pl.ds((first + t) * WIDE, TALL)]
            source = pieces[k].at[pl.ds(t * TALL, TALL)]
            return pltpu.make_async_copy(source, spot, sem.at[j, first + t])

        def fetch_strip(j):
            source = panel_ref.at[pl.ds(2 * index_ref[base + j], 2)]
            return pltpu.make_async_copy(source, strips.at[j], strip_sem.at[j, 0])

        def fetch_wide(j):
            source = wide_ref.at[index_ref[base + j]]
            return pltpu.make_async_copy(source, wides.at[j], strip_sem.at[j, 1])

        def fetch_more(k):
            return pltpu.make_async_copy(more[k], kept_more[k], more_sem.at[k])

        step = pl.program_id(0)

        @pl.when(step == 0)
        def _():
            for j in range(count):
                for one in halves:
                    if one[1] == j:
                        fetch(*one).start()
                fetch_strip(j).start()
                fetch_wide(j).start()
            for k in range(len(extra)):
                fetch_more(k).start()
            acc[...] = jnp.zeros_like(acc)
            gap = jnp.zeros((WIDE - TALL, WIDE), BF)
            for j in range(count):
                for t in range(2):
                    held[j, t * WIDE + TALL : (t + 1) * WIDE] = gap

        for j in range(count):

            @pl.when(step == j // 2)
            def _(j=j):
                fetch_strip(j).wait()
                fetch_wide(j).wait()
                for one in halves:
                    if one[1] == j:
                        fetch(*one).wait()

        for t in range(2):
            mask_rows(strips, wides, 2 * step + t, left, 2 * WIDE * t)
        right = held[pl.ds(2 * step, 2)].reshape(4 * WIDE, WIDE)
        if scaled:
            right = (right.astype(F32) * by).astype(BF)
        acc[...] += jnp.dot(left[...], right, preferred_element_type=F32)

        @pl.when(step == count // 2 - 1)
        def _():
            for k in range(len(extra)):
                fetch_more(k).wait()
            epilogue(acc, by, outs, *kept_more)

    whole = pl.BlockSpec(memory_space=pltpu.VMEM)
    smem = pl.BlockSpec(memory_space=pltpu.SMEM)
    anywhere = pl.BlockSpec(memory_space=pltpu.HBM)
    operands = [piece for _, piece in flat] + extra + list(early)
    return pl.pallas_call(
        body,
        out_shape=out_shape,
        grid=(count // 2,),
        in_specs=[smem, smem, anywhere, anywhere] + [anywhere] * len(operands),
        out_specs=[whole] * len(out_shape),
        scratch_shapes=[
            pltpu.VMEM((rows, WIDE), F32),
            pltpu.VMEM((count, 2 * WIDE, WIDE), BF),
            pltpu.VMEM((count, 2, rows, WIDE), BF),
            pltpu.VMEM((count,) + wide.shape[1:], F32),
            pltpu.VMEM((rows, 4 * WIDE), BF),
            pltpu.SemaphoreType.DMA((count, 2)),
            pltpu.SemaphoreType.DMA((count, 2)),
            pltpu.SemaphoreType.DMA((max(len(extra), 1),)),
        ]
        + [pltpu.VMEM(e.shape, e.dtype) for e in extra],
        compiler_params=pltpu.CompilerParams(vmem_limit_bytes=60 * 2**20),
        cost_estimate=pl.CostEstimate(
            flops=int(micros * 1.15e9), bytes_accessed=int(micros * 3e6), transcendentals=0
        ),
    )(index, scale, panel, wide, *operands)


def square_end(acc, by, outs, keep):
    for half in range(2):
        rows = slice(half * TALL, (half + 1) * TALL)
        outs[half][...] = (acc[rows] * keep[rows].astype(F32)).astype(BF)


def first_sum(acc, by, outs):
    outs[0][...] = acc[...]


def sign_end(acc, by, outs, so_far, keep, right, pack):
    first = (right[...].astype(F32) * by).astype(BF).astype(F32)
    cube = acc[...] + so_far[...]
    value = (keep[...].astype(F32) * (1.5 * first - 0.5 * cube)).astype(BF)
    outs[0][...] = jnp.dot(pack[...], value, preferred_element_type=F32).astype(BF)


def unpack_body(place_ref, arrived_ref, out_ref):
    value = jnp.dot(place_ref[...], arrived_ref[...], preferred_element_type=F32)
    out_ref[...] = value[:, : out_ref.shape[1]]


def after(ready, arrays):
    anywhere = pl.BlockSpec(memory_space=pl.ANY)
    return pl.pallas_call(
        lambda *refs: None,
        out_shape=[jax.ShapeDtypeStruct(a.shape, a.dtype) for a in arrays],
        in_specs=[anywhere] * (len(arrays) + 1),
        out_specs=[anywhere] * len(arrays),
        input_output_aliases={k + 1: k for k in range(len(arrays))},
    )(ready, *arrays)


def send(array, axis, by):
    return lax.ppermute(array, axis, shift(2 if axis == "c" else 4, by))


def from_all(array, axes, count):
    return lax.all_to_all(jnp.broadcast_to(array[None], (count,) + array.shape), axes, 0, 0)


PLACES = [(0, 0), (0, 1), (-1, 0), (1, 0), (-1, 1), (1, 1), (2, 0), (2, 1)]


def other(pieces):
    return tuple(send(piece, "c", 1) for piece in pieces)


def column_panel(block):
    before, behind = (send(block, "x", 1),), (send(block, "x", 3),)
    opposite = (send(before[0][:TALL], "x", 1), send(behind[0][TALL:], "x", 3))
    own = (block,)
    return [own, other(own), before, behind, other(before), other(behind), opposite, other(opposite)]


def column_panel_beside(top, bottom, beside):
    before_top, behind_bottom = send(top, "x", 1), send(bottom, "x", 3)
    before = (before_top, send(bottom, "x", 1))
    behind = (send(top, "x", 3), behind_bottom)
    opposite = [send(before_top, "x", 1), send(behind_bottom, "x", 3)]
    own = (top, bottom)
    partial = beside([own, other(own), before, behind])
    opposite = (after(partial, opposite[:1])[0], opposite[1])
    return [other(before), other(behind), opposite, other(opposite)], partial


def on_device(hamiltonian, new_atom, pattern):
    rows_here, cols_here = hamiltonian.shape
    row_count, col_count = 8, 16
    atoms_row, atoms_col = pattern.shape
    order_all = rows_here * row_count
    slots_col = -(-atoms_col // col_count)
    counts = np.bincount((1 + np.arange(atoms_col)) % col_count, minlength=col_count)
    targets = (np.arange(2)[:, None] + np.arange(col_count)[None, :]) % col_count // 2
    slots_row = max(int(np.sum((targets == t) * counts[None, :])) for t in range(row_count))
    x, c = lax.axis_index("x"), lax.axis_index("c")
    y, z = lax.axis_index("y"), lax.axis_index("z")
    row_here, col_here = 2 * x + c, 4 * y + z
    half = rows_here // 2
    pads = ((0, TALL - half), (0, WIDE - cols_here))
    padded = jnp.concatenate([jnp.pad(hamiltonian[:half], pads), jnp.pad(hamiltonian[half:], pads)])
    panel = lax.all_gather(padded, COL, axis=0)

    width = 32
    base = packed(new_atom, col_here, atoms_col, col_count, slots_col)
    spots = (base[:, :, None] * NBF + np.arange(NBF)).reshape(col_count, slots_col * NBF)
    column = jnp.pad(spots, ((0, 0), (0, width - slots_col * NBF)), constant_values=-1).reshape(-1)
    pick = eq(column[:, None], np.arange(WIDE)[None, :])
    outgoing = exact(pick, padded, (((1,), (1,)), ((), ())))
    arrived = lax.all_to_all(outgoing.reshape(col_count, width, 2 * TALL), COL, 0, 0)
    arrived = arrived.reshape(col_count * width, 2 * TALL)
    source, rank = arrivals(new_atom, col_here, atoms_col)
    spot = ((source * width + rank * NBF)[:, None] + np.arange(NBF)[None, :]).reshape(-1)
    spot = jnp.pad(spot, (0, WIDE - cols_here), constant_values=-1)
    place = eq(np.arange(col_count * width)[:, None], spot[None, :])
    moved = exact(arrived, place, (((0,), (0,)), ((), ())))

    strip = from_all(pattern.astype(BF), ROW, row_count).reshape(-1, atoms_col)
    old_row = row_here * atoms_row + np.arange(atoms_row)
    rows_pattern = exact(eq(old_row[:, None], new_atom[None, :]), strip)
    line = np.arange(2 * TALL) % TALL
    of_row = np.where(line < half, (np.arange(2 * TALL) // TALL * half + line) // NBF, -1)
    of_col = np.where(np.arange(WIDE) < cols_here, np.arange(WIDE) // NBF, -1)
    tall = eq(jnp.asarray(of_row)[:, None], np.arange(64)[None, :])
    broad = eq(np.arange(atoms_col)[:, None], jnp.asarray(of_col)[None, :])
    keep = exact(exact(tall[:, :atoms_row], rows_pattern), broad)
    right = moved * keep
    blocks = column_panel(right)

    part_sum = jnp.sum(jnp.square(right.astype(F32)))
    sent = jnp.concatenate(
        [rows_pattern.astype(F32), jnp.broadcast_to(part_sum, (8, atoms_col))], axis=0
    )
    seen = from_all(sent, COL, col_count)
    total = jnp.broadcast_to(jnp.sum(seen[:, atoms_row, 0]), (8, 128))
    total = jnp.sum(from_all(total, ROW, row_count), axis=0)
    scale = lax.rsqrt(total[:1, :1] / order_all)
    all_cols = jnp.transpose(seen[:, :atoms_row], (1, 0, 2)).reshape(atoms_row, -1).astype(BF)
    old_col = np.where(of_col >= 0, np.arange(col_count)[:, None] * atoms_col + of_col, -1)
    old_col = jnp.asarray(old_col.reshape(row_count, 1, 2 * WIDE))
    wide = scale * jnp.einsum(
        "ia,ran->rin", all_cols, eq(new_atom[None, :, None], old_col), preferred_element_type=F32
    )

    def rho(step, other_core):
        return 2 * jnp.mod(x + step, 4) + jnp.mod(c + other_core, 2)

    index = jnp.stack([rho(d, o) for d, o in PLACES])
    sums = jax.ShapeDtypeStruct((2 * TALL, WIDE), F32)
    whole = pl.BlockSpec(memory_space=pltpu.VMEM)
    of_panel = functools.partial(multiply, panel, wide, scale, index)
    base = packed(new_atom, row_here, atoms_row, row_count, slots_row)
    line = (base[:, :, None] * NBF + np.arange(NBF)).reshape(-1)
    row_of = np.where(of_row >= 0, np.arange(2 * TALL) - (np.arange(2 * TALL) // TALL) * (TALL - half), -1)
    pack_rows = eq(line[:, None], jnp.asarray(row_of)[None, :])
    half_block = jax.ShapeDtypeStruct((TALL, WIDE), BF)
    square = of_panel(0, blocks, True, square_end, [keep], [half_block] * 2, 9, [pack_rows])
    blocks, partial = column_panel_beside(
        *square,
        lambda first: of_panel(0, first, False, first_sum, [], [sums], 7)[0],
    )
    sent_rows = of_panel(
        4, blocks, False, sign_end, [partial, keep, right, pack_rows],
        [jax.ShapeDtypeStruct((row_count * slots_row * NBF, WIDE), BF)], 9,
    )[0]
    got_rows = lax.all_to_all(sent_rows.reshape(row_count, slots_row * NBF, WIDE), ROW, 0, 0)
    got_rows = got_rows.reshape(-1, WIDE)
    source, rank = arrivals(new_atom, row_here, atoms_row)
    spot = (((source * slots_row + rank) * NBF)[:, None] + np.arange(NBF)).reshape(-1)
    place_rows = eq(spot[:, None], np.arange(row_count * slots_row * NBF)[None, :])
    return pl.pallas_call(
        unpack_body,
        out_shape=jax.ShapeDtypeStruct((rows_here, cols_here), F32),
        in_specs=[whole, whole],
        out_specs=whole,
    )(place_rows, got_rows)


def solution(mesh):
    split = Mesh(mesh.devices.reshape(4, 2, 4, 4), ("x", "c", "y", "z"))
    return jax.shard_map(
        on_device,
        mesh=split,
        in_specs=(P(ROW, COL), P(), P(ROW, COL)),
        out_specs=P(ROW, COL),
        check_vma=False,
    )
```

```python
import functools

import jax
import jax.numpy as jnp
import numpy as np
from jax import lax
from jax.experimental import pallas as pl
from jax.experimental.pallas import tpu as pltpu
from jax.sharding import Mesh
from jax.sharding import PartitionSpec as P

NBF = 13
ROW = ("x", "c")
COL = ("y", "z")
BF = jnp.bfloat16
F32 = jnp.float32


def shift(n, by):
    return [(i, (i + by) % n) for i in range(n)]


def eq(left, right):
    return (left == right).astype(BF)


def exact(left, right, dims=(((1,), (0,)), ((), ()))):
    return lax.dot_general(left, right, dims, preferred_element_type=F32).astype(BF)


def slots_of(source, groups, per_group):
    same = source[:, :, None] == source[:, None, :]
    earlier = np.tril(np.ones((per_group, per_group), bool), -1)
    return jnp.sum((same & earlier[None]).astype(jnp.int32), axis=2)


def packed(new_atom, here, per_block, groups, slots):
    table = new_atom.reshape(groups, per_block)
    source = table // per_block
    rank = slots_of(source, groups, per_block)
    hit = (source == here)[:, None, :] & (rank[:, None, :] == np.arange(slots)[None, :, None])
    return jnp.sum(jnp.where(hit, (table - here * per_block)[:, None, :] + 1000, 0), axis=2) - 1000


def arrivals(new_atom, here, per_block):
    table = lax.dynamic_slice_in_dim(new_atom, here * per_block, per_block)
    source = table // per_block
    return source, slots_of(source[None], 1, per_block)[0]


TALL = 368
WIDE = 384


def mask_rows(strips, wides, step, left, first_column):
    columns = 2 * WIDE
    line = lax.broadcasted_iota(jnp.int32, (8, columns), 0)
    in_half = wides.shape[1] // 2

    def of_atom(half, atom):
        return jnp.broadcast_to(wides[step, pl.ds(half * in_half + atom, 1), :], (8, columns))

    for start in range(0, left.shape[0], 16):
        masks = []
        for first in (start, start + 8):
            half, row = divmod(first, TALL)
            atom, more = divmod(row, NBF)
            here = NBF - more
            mask = of_atom(half, atom)
            if here < 8:
                mask = jnp.where(line < here, mask, of_atom(half, atom + 1) if atom + 1 < in_half else 0.0)
            masks.append(mask)
        rows = pl.ds(start, 16)
        both = jnp.concatenate([strips[step, 0, rows], strips[step, 1, rows]], axis=1)
        left[rows, first_column : first_column + columns] = (both.astype(F32) * jnp.concatenate(masks, axis=0)).astype(BF)


def multiply(panel, wide, scale, index, base, blocks, scaled, epilogue, extra, out_shape, micros, early=()):
    count = len(blocks)
    rows = panel.shape[1]
    flat = [(j, piece) for j, pieces in enumerate(blocks) for piece in pieces]
    starts = [sum(p.shape[0] for _, p in flat[:k]) for k in range(len(flat))]
    halves = [
        (k, j, (at - 2 * TALL * j) // TALL, t)
        for k, ((j, piece), at) in enumerate(zip(flat, starts))
        for t in range(piece.shape[0] // TALL)
    ]

    def body(index_ref, scale_ref, panel_ref, wide_ref, *refs):
        pieces, refs = refs[: len(flat)], refs[len(flat) :]
        more, refs = refs[: len(extra)], refs[len(extra) + len(early) :]
        outs, refs = refs[: len(out_shape)], refs[len(out_shape) :]
        acc, held, strips, wides, left, sem, strip_sem, more_sem = refs[:8]
        kept_more = refs[8:]
        by = scale_ref[0, 0]

        def fetch(k, j, first, t):
            spot = held.at[j, pl.ds((first + t) * WIDE, TALL)]
            source = pieces[k].at[pl.ds(t * TALL, TALL)]
            return pltpu.make_async_copy(source, spot, sem.at[j, first + t])

        def fetch_strip(j):
            source = panel_ref.at[pl.ds(2 * index_ref[base + j], 2)]
            return pltpu.make_async_copy(source, strips.at[j], strip_sem.at[j, 0])

        def fetch_wide(j):
            source = wide_ref.at[index_ref[base + j]]
            return pltpu.make_async_copy(source, wides.at[j], strip_sem.at[j, 1])

        def fetch_more(k):
            return pltpu.make_async_copy(more[k], kept_more[k], more_sem.at[k])

        step = pl.program_id(0)

        @pl.when(step == 0)
        def _():
            for j in range(count):
                for one in halves:
                    if one[1] == j:
                        fetch(*one).start()
                fetch_strip(j).start()
                fetch_wide(j).start()
            for k in range(len(extra)):
                fetch_more(k).start()
            acc[...] = jnp.zeros_like(acc)
            gap = jnp.zeros((WIDE - TALL, WIDE), BF)
            for j in range(count):
                for t in range(2):
                    held[j, t * WIDE + TALL : (t + 1) * WIDE] = gap

        for j in range(count):

            @pl.when(step == j // 2)
            def _(j=j):
                fetch_strip(j).wait()
                fetch_wide(j).wait()
                for one in halves:
                    if one[1] == j:
                        fetch(*one).wait()

        for t in range(2):
            mask_rows(strips, wides, 2 * step + t, left, 2 * WIDE * t)
        right = held[pl.ds(2 * step, 2)].reshape(4 * WIDE, WIDE)
        if scaled:
            right = (right.astype(F32) * by).astype(BF)
        acc[...] += jnp.dot(left[...], right, preferred_element_type=F32)

        @pl.when(step == count // 2 - 1)
        def _():
            for k in range(len(extra)):
                fetch_more(k).wait()
            epilogue(acc, by, outs, *kept_more)

    whole = pl.BlockSpec(memory_space=pltpu.VMEM)
    smem = pl.BlockSpec(memory_space=pltpu.SMEM)
    anywhere = pl.BlockSpec(memory_space=pltpu.HBM)
    operands = [piece for _, piece in flat] + extra + list(early)
    return pl.pallas_call(
        body,
        out_shape=out_shape,
        grid=(count // 2,),
        in_specs=[smem, smem, anywhere, anywhere] + [anywhere] * len(operands),
        out_specs=[whole] * len(out_shape),
        scratch_shapes=[
            pltpu.VMEM((rows, WIDE), F32),
            pltpu.VMEM((count, 2 * WIDE, WIDE), BF),
            pltpu.VMEM((count, 2, rows, WIDE), BF),
            pltpu.VMEM((count,) + wide.shape[1:], F32),
            pltpu.VMEM((rows, 4 * WIDE), BF),
            pltpu.SemaphoreType.DMA((count, 2)),
            pltpu.SemaphoreType.DMA((count, 2)),
            pltpu.SemaphoreType.DMA((max(len(extra), 1),)),
        ]
        + [pltpu.VMEM(e.shape, e.dtype) for e in extra],
        compiler_params=pltpu.CompilerParams(vmem_limit_bytes=60 * 2**20),
        cost_estimate=pl.CostEstimate(
            flops=int(micros * 1.15e9), bytes_accessed=int(micros * 3e6), transcendentals=0
        ),
    )(index, scale, panel, wide, *operands)


def square_end(acc, by, outs, keep):
    for half in range(2):
        rows = slice(half * TALL, (half + 1) * TALL)
        outs[half][...] = (acc[rows] * keep[rows].astype(F32)).astype(BF)


def first_sum(acc, by, outs):
    outs[0][...] = acc[...]


def sign_end(acc, by, outs, so_far, keep, right, pack):
    first = (right[...].astype(F32) * by).astype(BF).astype(F32)
    cube = acc[...] + so_far[...]
    value = (keep[...].astype(F32) * (1.5 * first - 0.5 * cube)).astype(BF)
    outs[0][...] = jnp.dot(pack[...], value, preferred_element_type=F32).astype(BF)


def after(ready, arrays):
    anywhere = pl.BlockSpec(memory_space=pl.ANY)
    return pl.pallas_call(
        lambda *refs: None,
        out_shape=[jax.ShapeDtypeStruct(a.shape, a.dtype) for a in arrays],
        in_specs=[anywhere] * (len(arrays) + 1),
        out_specs=[anywhere] * len(arrays),
        input_output_aliases={k + 1: k for k in range(len(arrays))},
    )(ready, *arrays)


def send(array, axis, by):
    return lax.ppermute(array, axis, shift(2 if axis == "c" else 4, by))


def from_all(array, axes, count):
    return lax.all_to_all(jnp.broadcast_to(array[None], (count,) + array.shape), axes, 0, 0)


PLACES = [(0, 0), (0, 1), (-1, 0), (1, 0), (-1, 1), (1, 1), (2, 0), (2, 1)]


def other(pieces):
    return tuple(send(piece, "c", 1) for piece in pieces)


def column_panel(block):
    before, behind = (send(block, "x", 1),), (send(block, "x", 3),)
    opposite = (send(before[0][:TALL], "x", 1), send(behind[0][TALL:], "x", 3))
    own = (block,)
    return [own, other(own), before, behind, other(before), other(behind), opposite, other(opposite)]


def column_panel_beside(top, bottom, beside):
    before_top, behind_bottom = send(top, "x", 1), send(bottom, "x", 3)
    before = (before_top, send(bottom, "x", 1))
    behind = (send(top, "x", 3), behind_bottom)
    opposite = [send(before_top, "x", 1), send(behind_bottom, "x", 3)]
    own = (top, bottom)
    partial = beside([own, other(own), before, behind])
    opposite = (after(partial, opposite[:1])[0], opposite[1])
    return [other(before), other(behind), opposite, other(opposite)], partial


def on_device(hamiltonian, new_atom, pattern):
    rows_here, cols_here = hamiltonian.shape
    row_count, col_count = 8, 16
    atoms_row, atoms_col = pattern.shape
    order_all = rows_here * row_count
    slots_col = -(-atoms_col // col_count)
    counts = np.bincount((1 + np.arange(atoms_col)) % col_count, minlength=col_count)
    targets = (np.arange(2)[:, None] + np.arange(col_count)[None, :]) % col_count // 2
    slots_row = max(int(np.sum((targets == t) * counts[None, :])) for t in range(row_count))
    x, c = lax.axis_index("x"), lax.axis_index("c")
    y, z = lax.axis_index("y"), lax.axis_index("z")
    row_here, col_here = 2 * x + c, 4 * y + z
    half = rows_here // 2
    pads = ((0, TALL - half), (0, WIDE - cols_here))
    padded = jnp.concatenate([jnp.pad(hamiltonian[:half], pads), jnp.pad(hamiltonian[half:], pads)])
    panel = lax.all_gather(padded, COL, axis=0)

    width = 32
    base = packed(new_atom, col_here, atoms_col, col_count, slots_col)
    spots = (base[:, :, None] * NBF + np.arange(NBF)).reshape(col_count, slots_col * NBF)
    column = jnp.pad(spots, ((0, 0), (0, width - slots_col * NBF)), constant_values=-1).reshape(-1)
    pick = eq(column[:, None], np.arange(WIDE)[None, :])
    outgoing = exact(pick, padded, (((1,), (1,)), ((), ())))
    arrived = lax.all_to_all(outgoing.reshape(col_count, width, 2 * TALL), COL, 0, 0)
    arrived = arrived.reshape(col_count * width, 2 * TALL)
    source, rank = arrivals(new_atom, col_here, atoms_col)
    spot = ((source * width + rank * NBF)[:, None] + np.arange(NBF)[None, :]).reshape(-1)
    spot = jnp.pad(spot, (0, WIDE - cols_here), constant_values=-1)
    place = eq(np.arange(col_count * width)[:, None], spot[None, :])
    moved = exact(arrived, place, (((0,), (0,)), ((), ())))

    strip = from_all(pattern.astype(BF), ROW, row_count).reshape(-1, atoms_col)
    old_row = row_here * atoms_row + np.arange(atoms_row)
    rows_pattern = exact(eq(old_row[:, None], new_atom[None, :]), strip)
    line = np.arange(2 * TALL) % TALL
    of_row = np.where(line < half, (np.arange(2 * TALL) // TALL * half + line) // NBF, -1)
    of_col = np.where(np.arange(WIDE) < cols_here, np.arange(WIDE) // NBF, -1)
    tall = eq(jnp.asarray(of_row)[:, None], np.arange(64)[None, :])
    broad = eq(np.arange(atoms_col)[:, None], jnp.asarray(of_col)[None, :])
    keep = exact(exact(tall[:, :atoms_row], rows_pattern), broad)
    right = moved * keep
    blocks = column_panel(right)

    part_sum = jnp.sum(jnp.square(right.astype(F32)))
    sent = jnp.concatenate(
        [rows_pattern.astype(F32), jnp.broadcast_to(part_sum, (8, atoms_col))], axis=0
    )
    seen = from_all(sent, COL, col_count)
    total = jnp.broadcast_to(jnp.sum(seen[:, atoms_row, 0]), (8, 128))
    total = jnp.sum(from_all(total, ROW, row_count), axis=0)
    scale = lax.rsqrt(total[:1, :1] / order_all)
    all_cols = jnp.transpose(seen[:, :atoms_row], (1, 0, 2)).reshape(atoms_row, -1).astype(BF)
    old_col = np.where(of_col >= 0, np.arange(col_count)[:, None] * atoms_col + of_col, -1)
    old_col = jnp.asarray(old_col.reshape(row_count, 1, 2 * WIDE))
    wide = scale * jnp.einsum(
        "ia,ran->rin", all_cols, eq(new_atom[None, :, None], old_col), preferred_element_type=F32
    )

    def rho(step, other_core):
        return 2 * jnp.mod(x + step, 4) + jnp.mod(c + other_core, 2)

    index = jnp.stack([rho(d, o) for d, o in PLACES])
    sums = jax.ShapeDtypeStruct((2 * TALL, WIDE), F32)
    whole = pl.BlockSpec(memory_space=pltpu.VMEM)
    of_panel = functools.partial(multiply, panel, wide, scale, index)
    base = packed(new_atom, row_here, atoms_row, row_count, slots_row)
    line = (base[:, :, None] * NBF + np.arange(NBF)).reshape(-1)
    row_of = np.where(of_row >= 0, np.arange(2 * TALL) - (np.arange(2 * TALL) // TALL) * (TALL - half), -1)
    pack_rows = eq(line[:, None], jnp.asarray(row_of)[None, :])
    half_block = jax.ShapeDtypeStruct((TALL, WIDE), BF)
    square = of_panel(0, blocks, True, square_end, [keep], [half_block] * 2, 9, [pack_rows])
    blocks, partial = column_panel_beside(
        *square,
        lambda first: of_panel(0, first, False, first_sum, [], [sums], 7)[0],
    )
    sent_rows = of_panel(
        4, blocks, False, sign_end, [partial, keep, right, pack_rows],
        [jax.ShapeDtypeStruct((row_count * slots_row * NBF, WIDE), BF)], 9,
    )[0]
    got_rows = lax.all_to_all(sent_rows.reshape(row_count, slots_row * NBF, WIDE), ROW, 0, 0)
    got_rows = got_rows.reshape(-1, WIDE)
    source, rank = arrivals(new_atom, row_here, atoms_row)
    spot = (((source * slots_row + rank) * NBF)[:, None] + np.arange(NBF)).reshape(-1)
    place_rows = eq(spot[:, None], np.arange(row_count * slots_row * NBF)[None, :])
    return jnp.dot(place_rows, got_rows[:, :cols_here], preferred_element_type=F32)


def solution(mesh):
    split = Mesh(mesh.devices.reshape(4, 2, 4, 4), ("x", "c", "y", "z"))
    return jax.shard_map(
        on_device,
        mesh=split,
        in_specs=(P(ROW, COL), P(), P(ROW, COL)),
        out_specs=P(ROW, COL),
        check_vma=False,
    )
```
